32 devices in a mesh: sec: 8 (over z, core), term: 4 (over y, x).
Axes of the slice: x: 2, y: 2, z: 4, core: 2. Of those that a mesh axis runs over, the one named last changes fastest.
Arguments:
- psi: bfloat16 [32, 4, 256, 256], P('sec'), may hold values from -6 to 6
- left_env: bfloat16 [16, 32, 256, 256], P('term', 'sec'), may hold values from -0.09375 to 0.09375
- right_env: bfloat16 [16, 256, 256], P('term'), may hold values from -0.375 to 0.375
- site_ops: float32 [16, 4, 4], P('term'), may hold values from -3 to 3
- coupling: int32 [16, 32], P('term', 'sec'), may hold values from -1 to 31, as said below
- live: int32 [32], P('sec'), may hold values from 128 to 256, as said below
Outputs:
- sigma: bfloat16 [32, 4, 256, 256], P('sec', None, 'term')
The draws below stay inside these ranges and needn't reach their ends.
Inputs may be any that keep to these rules, and one draw needn't show every extreme that they name: coupling[t, s] is -1 or a block within 2 of s; some terms couple at distance 2 in both directions. live sizes are at least 128.
All inputs are finite; a program needn't handle non-finite values.
Results may differ from the reference program's by a relative error of at most 0.018.
Values may be sent and summed in bfloat16 or wider, within the bound.
No kernel may reach another device: no remote copies, remote signals or barrier semaphores. Data moves between devices by JAX's collectives and lax.ppermute only.
A program may use at most 64 MiB of HBM per device.

```python
import jax
import jax.numpy as jnp
from jax import lax

B = 256
K = 4
NS = 32
TERMS = 16


def draw_coupling(key, part):
    shift_key = jax.random.fold_in(key, 11)
    keep_key = jax.random.fold_in(key, 12)
    shifts = jax.random.randint(shift_key, (TERMS,), -2, 3)
    shifts = shifts.at[0].set(2)
    shifts = shifts.at[1].set(-2)
    target = jnp.arange(NS, dtype=jnp.int32)[None, :] + shifts[:, None]
    keeper = jax.random.randint(keep_key, (TERMS, NS), 0, 5) > 0
    valid = (target >= 0) & (target < NS) & keeper
    return jnp.where(valid, target, -1).astype(jnp.int32)


def draw_live(key, part):
    sizes = jax.random.randint(jax.random.fold_in(key, 21), (NS,), B // 2, B + 1)
    return sizes.at[0].set(B).astype(jnp.int32)


def shard_levels(own_key, extent, pieces, low, high):
    level = 1.0
    for axis_at, parts in pieces:
        draws = jax.random.uniform(jax.random.fold_in(jax.random.fold_in(own_key, 6), axis_at), (parts,), jnp.float32, low / len(pieces), high / len(pieces))
        level = level * jnp.repeat(jnp.exp(draws), extent[axis_at] // parts).reshape((-1,) + (1,) * (len(extent) - 1 - axis_at))
    return level


def gaussian(rng, extent, deviation, reach, pieces=(), kind=jnp.bfloat16):
    gain = shard_levels(rng, extent, pieces, -0.22, 0.18) if pieces else 1.0
    values = jax.random.normal(rng, extent, jnp.float32) * deviation * gain
    return jnp.minimum(jnp.maximum(values, -reach), reach).astype(kind)


def setup_inputs(seed: int = 0) -> dict:
    seeds = jax.random.split(jax.random.key(seed), 7)
    return {
        "psi": gaussian(seeds[0], (NS, K, B, B), 1.0, 6.0, ((0, 8),)),
        "left_env": gaussian(seeds[1], (TERMS, NS, B, B), (B * TERMS) ** -0.5, 0.09375, ((0, 4), (1, 8))),
        "right_env": gaussian(seeds[2], (TERMS, B, B), B ** -0.5, 0.375, ((0, 4),)),
        "site_ops": gaussian(seeds[3], (TERMS, K, K), K ** -0.5, 3.0, ((0, 4),), jnp.float32),
        "coupling": draw_coupling(jax.random.fold_in(seeds[6], 71), 0),
        "live": draw_live(jax.random.fold_in(seeds[6], 71), 0),
    }


def reference(psi, left_env, right_env, site_ops, coupling, live):
    width = psi.shape[2]

    def term_step(acc, inputs):
        left_t, right_t, ops_t, couple_t = inputs
        valid = couple_t >= 0
        index = jnp.where(valid, couple_t, 0).astype(jnp.int32)
        source = psi[index]
        mixed = jnp.einsum('kj,sjab->skab', ops_t.astype(jnp.float32), source.astype(jnp.float32))
        mixed = (mixed * valid[:, None, None, None].astype(jnp.float32)).astype(jnp.bfloat16)
        inner = jnp.einsum('sab,skbc->skac', left_t.astype(jnp.float32), mixed.astype(jnp.float32)).astype(jnp.bfloat16)
        outer = jnp.einsum('skac,cd->skad', inner.astype(jnp.float32), right_t.astype(jnp.float32))
        return acc + outer, None

    start = jnp.zeros(psi.shape, jnp.float32)
    total, unused = lax.scan(term_step, start, (left_env, right_env, site_ops, coupling))
    position = jnp.arange(width, dtype=jnp.int32)
    rows_ok = position[None, :] < live[:, None]
    keep = rows_ok[:, :, None] & rows_ok[:, None, :]
    result = jnp.where(keep[:, None, :, :], total, 0.0)
    return result.astype(jnp.bfloat16)
```

```python
import functools

import jax
import jax.numpy as jnp
from jax import lax
from jax.experimental import pallas as pl
from jax.experimental.pallas import tpu as pltpu
from jax.sharding import PartitionSpec as P

VMEM_LIMIT = 40 * 1024 * 1024


def flip(value, bit):
    size = lax.axis_size("term")
    return lax.ppermute(value, "term", [(i, i ^ bit) for i in range(size)])


def apply_body(firsts, facing, orders, info, couple, ops, psi, left, right, *refs):
    extras, rest = refs[: -(2 * len(orders) + 6)], refs[-(2 * len(orders) + 6) :]
    outs, (ext, lv, rv, mixed, inner, sems) = rest[: 2 * len(orders)], rest[2 * len(orders) :]
    terms, width = right.shape[0], right.shape[1]
    states = ops.shape[1]
    count = len(firsts[0])
    own = psi.shape[0]
    devices = len(orders[0])
    rows = width // devices
    base, odd, me = info[0], info[1], info[2]

    def block_of(n):
        return jnp.where(odd == 1, firsts[1][n], firsts[0][n])

    copies = [pltpu.make_async_copy(psi, ext.at[pl.ds(0, own)], sems.at[0])]
    at = own
    for extra in extras:
        copies.append(pltpu.make_async_copy(extra, ext.at[pl.ds(at, extra.shape[0])], sems.at[1 + at - own]))
        at += extra.shape[0]
    slots = at
    for n in range(count):
        for i in range(devices):
            copies.append(
                pltpu.make_async_copy(
                    left.at[:, block_of(n), pl.ds(pl.multiple_of((i ^ me) * rows, rows), rows), :],
                    lv.at[n, :, pl.ds(i * rows, rows), :],
                    sems.at[4 + n * devices + i],
                )
            )
    copies.append(pltpu.make_async_copy(right, rv, sems.at[3]))
    for copy in copies:
        copy.start()
    for copy in copies:
        copy.wait()

    for n in range(count):
        s = block_of(n)
        for t in range(terms):
            c = couple[t, s]
            valid = jnp.where(c >= 0, 1.0, 0.0).astype(jnp.float32)
            r = c - base
            if facing:
                other = jnp.where(odd == 1, r + own + 2, r)
            else:
                other = jnp.where(odd == 1, r, own - 1 - r)
            slot = jnp.where((r >= 0) & (r < own), r, other)
            slot = jnp.clip(jnp.where(c >= 0, slot, 0), 0, slots - 1)
            coef = [[ops[t, k, j] * valid for j in range(states)] for k in range(states)]
            for a in range(0, width, 16):
                source = [ext[slot, j, a : a + 16, :].astype(jnp.float32) for j in range(states)]
                for k in range(states):
                    value = coef[k][0] * source[0]
                    for j in range(1, states):
                        value = value + coef[k][j] * source[j]
                    mixed[t % 2, a : a + 16, k * width : (k + 1) * width] = value.astype(jnp.bfloat16)
            value = jnp.dot(lv[n, t], mixed[t % 2], preferred_element_type=jnp.float32)
            for k in range(states):
                inner[k * width : (k + 1) * width, t * width : (t + 1) * width] = value[
                    :, k * width : (k + 1) * width
                ].astype(jnp.bfloat16)
        for k in range(states):
            value = jnp.dot(
                inner[k * width : (k + 1) * width, :],
                rv[...].reshape(terms * width, width),
                preferred_element_type=jnp.float32,
            ).astype(jnp.bfloat16)
            path = k * len(orders) // states
            kk = k % (states // len(orders))
            keep, send = outs[2 * path], outs[2 * path + 1]
            half = devices // 2
            for at, i in enumerate(orders[path]):
                target = keep if at < half else send
                target[at % half, n, kk] = value[i * rows : (i + 1) * rows, :]


def apply_blocks(firsts, facing, orders, info, couple, ops, psi, left, right, extras):
    terms, width = right.shape[0], right.shape[1]
    states = ops.shape[1]
    count = len(firsts[0])
    devices = len(orders[0])
    rows = width // devices
    paths = len(orders)
    part = jax.ShapeDtypeStruct((devices // 2, count, states // paths, rows, width), jnp.bfloat16)
    smem = pl.BlockSpec(memory_space=pltpu.SMEM)
    hbm = pl.BlockSpec(memory_space=pl.ANY)
    vmem = pl.BlockSpec(memory_space=pltpu.VMEM)
    slots = psi.shape[0] + sum(e.shape[0] for e in extras)
    pairs = count * terms
    return pl.pallas_call(
        functools.partial(apply_body, firsts, facing, orders),
        out_shape=[part] * (2 * paths),
        in_specs=[smem] * 3 + [hbm] * (3 + len(extras)),
        out_specs=[vmem] * (2 * paths),
        scratch_shapes=[
            pltpu.VMEM((slots,) + psi.shape[1:], jnp.bfloat16),
            pltpu.VMEM((count, terms, width, width), jnp.bfloat16),
            pltpu.VMEM((terms, width, width), jnp.bfloat16),
            pltpu.VMEM((2, width, states * width), jnp.bfloat16),
            pltpu.VMEM((states * width, terms * width), jnp.bfloat16),
            pltpu.SemaphoreType.DMA((4 + count * devices,)),
        ],
        compiler_params=pltpu.CompilerParams(vmem_limit_bytes=VMEM_LIMIT),
        cost_estimate=pl.CostEstimate(
            flops=pairs * states * 4 * width**3, bytes_accessed=4 * 1024 * 1024, transcendentals=0
        ),
        name=f"apply_{'facing' if facing else 'outer'}_{count}",
    )(info, couple, ops, psi, left, right, *extras)


def finish_body(firsts, info, live, *refs):
    out = refs[-1]
    odd, me = info[1], info[2]
    rows, width = out.shape[2], out.shape[3]
    at = 0
    for group in firsts:
        count = len(group[0])
        for path in range(2):
            keep, first, last = refs[at : at + 3]
            at += 3
            kh = keep.shape[2]
            for n in range(count):
                s = jnp.where(odd == 1, group[1][n], group[0][n])
                size = live[s]
                row = lax.broadcasted_iota(jnp.int32, (rows, width), 0) + me * rows
                col = lax.broadcasted_iota(jnp.int32, (rows, width), 1)
                ok = (row < size) & (col < size)
                for kk in range(kh):
                    value = keep[0, n, kk].astype(jnp.float32) + first[0, n, kk].astype(jnp.float32)
                    value = value + last[0, n, kk].astype(jnp.float32)
                    out[s, path * kh + kk] = jnp.where(ok, value, 0.0).astype(jnp.bfloat16)


def finish(firsts, info, live, parts, shape):
    smem = pl.BlockSpec(memory_space=pltpu.SMEM)
    vmem = pl.BlockSpec(memory_space=pltpu.VMEM)
    return pl.pallas_call(
        functools.partial(finish_body, firsts),
        out_shape=jax.ShapeDtypeStruct(shape, jnp.bfloat16),
        in_specs=[smem] * 2 + [vmem] * len(parts),
        out_specs=vmem,
        compiler_params=pltpu.CompilerParams(vmem_limit_bytes=VMEM_LIMIT),
        name="finish",
    )(info, live, *parts)


def on_device(psi, left, right, ops, couple, live):
    secs, devices = lax.axis_size("sec"), lax.axis_size("term")
    sec, term = lax.axis_index("sec"), lax.axis_index("term")
    own, states, width = psi.shape[0], psi.shape[1], psi.shape[2]
    odd = sec % 2
    info = jnp.stack([sec * own, odd, term]).astype(jnp.int32)

    bits = [1 << b for b in range(devices.bit_length() - 1)]
    paths = (bits, bits[::-1])
    orders = tuple(
        tuple(sorted(range(devices), key=lambda i: [bool(i & b) for b in path])) for path in paths
    )

    chip = [(i, i ^ 1) for i in range(secs)]
    link = [(i, i + 1) for i in range(1, secs - 1, 2)]
    link = link + [(j, i) for i, j in link]
    facing_send = lax.dynamic_slice_in_dim(psi, (1 - odd) * 2, 2, 0)
    near_send = lax.dynamic_slice_in_dim(psi, odd * 3, 1, 0)
    far_send = lax.dynamic_slice_in_dim(psi, 1 + odd, 1, 0)
    inside = lax.ppermute(facing_send, "sec", chip)
    near = lax.ppermute(near_send, "sec", link)
    far = lax.ppermute(far_send, "sec", link)

    groups = (((2, 3), (0, 1)), ((1,), (2,)), ((0,), (3,)))
    extras = ((inside,), (near,), (near, far))
    parts = []
    for g, group in enumerate(groups):
        made = apply_blocks(group, g == 0, orders, info, couple, ops, psi, left, right, extras[g])
        for p, path in enumerate(paths):
            keep, send = made[2 * p], made[2 * p + 1]
            got = flip(send, path[0])
            for bit in path[1:-1]:
                half = keep.shape[0] // 2
                total = keep + got
                keep, send = total[:half], total[half:]
                got = flip(send, bit)
            send = keep[1:] + got[1:]
            parts += [keep[:1], got[:1], flip(send, path[-1])]
    shape = (own, states, width // devices, width)
    return finish(groups, info, live, parts, shape)


def solution(mesh):
    placed = (
        P("sec", None, None, None),
        P("term", "sec", None, None),
        P("term", None, None),
        P("term", None, None),
        P("term", "sec"),
        P("sec"),
    )
    return jax.shard_map(
        on_device,
        mesh=mesh,
        in_specs=placed,
        out_specs=P("sec", None, "term", None),
        check_vma=False,
    )
```

```python
import functools

import jax
import jax.numpy as jnp
from jax import lax
from jax.experimental import pallas as pl
from jax.experimental.pallas import tpu as pltpu
from jax.sharding import PartitionSpec as P

VMEM_LIMIT = 24 * 1024 * 1024
COST = 10


def flip(value, routes, step):
    secs, devices = lax.axis_size("sec"), lax.axis_size("term")
    pairs = []
    for sec in range(secs):
        for term in range(devices):
            pairs.append((sec * devices + term, sec * devices + (term ^ routes[sec % 2][step])))
    return lax.ppermute(value, ("sec", "term"), pairs)


def over_link(value, bit):
    secs, devices = lax.axis_size("sec"), lax.axis_size("term")
    pairs = []
    for sec in range(secs):
        other = sec + 1 if sec % 2 else sec - 1
        for term in range(devices):
            to = other * devices + term if 0 <= other < secs else sec * devices + (term ^ bit)
            pairs.append((sec * devices + term, to))
    return lax.ppermute(value, ("sec", "term"), pairs)


def pick_body(psi, right, own, rv, *refs):
    outs, sems = refs[:-1], refs[-1]
    odd = lax.axis_index("sec") % 2
    copies = [pltpu.make_async_copy(psi, own, sems.at[0]), pltpu.make_async_copy(right, rv, sems.at[1])]
    for copy in copies:
        copy.start()
    copies[0].wait()
    last = psi.shape[0] - 1
    for out, even in zip(outs, (last, last - 1, 0, 1)):
        out[...] = own[pl.ds(jnp.where(odd == 1, last - even, even), 1)]
    copies[1].wait()


def pick(psi, right):
    vmem = pl.BlockSpec(memory_space=pltpu.VMEM)
    hbm = pl.BlockSpec(memory_space=pltpu.HBM)
    shapes = [pltpu.VMEM(psi.shape, psi.dtype), pltpu.VMEM(right.shape, right.dtype)]
    shapes += [pltpu.VMEM((1,) + psi.shape[1:], psi.dtype)] * 4
    return pl.pallas_call(
        pick_body,
        out_shape=shapes,
        in_specs=[hbm, hbm],
        out_specs=[vmem] * 6,
        scratch_shapes=[pltpu.SemaphoreType.DMA((2,))],
        compiler_params=pltpu.CompilerParams(vmem_limit_bytes=VMEM_LIMIT),
        name="pick",
    )(*(pltpu.with_memory_space_constraint(v, pltpu.HBM) for v in (psi, right)))


def entry(table, *at):
    here = True
    for axis, index in enumerate(at):
        here = here & (lax.broadcasted_iota(jnp.int32, table.shape, axis) == index)
    return jnp.sum(jnp.where(here, table.astype(jnp.float32), 0.0)).astype(jnp.int32)


def apply_body(blocks, facing, orders, couple, ops, left, rv, own, *refs):
    extras, (keep, send, mixed, inner, total) = refs[:-5], refs[-5:]
    terms, width = rv.shape[0], rv.shape[1]
    count, states = own.shape[0], own.shape[1]
    devices = len(orders[0])
    half = devices // 2
    rows = width // devices
    sec, me = lax.axis_index("sec"), lax.axis_index("term")
    base, odd = sec * count, sec % 2
    strip = 16

    for n, block in enumerate(blocks):
        s = jnp.where(odd == 1, block[1], block[0])
        for t in range(terms):
            c = entry(couple[...], t, s)
            valid = jnp.where(c >= 0, 1.0, 0.0).astype(jnp.float32)
            r = jnp.where(c >= 0, c - base, 0)
            halo = jnp.where((odd == 1) == facing, -1 - r, r - count)
            inside = (r >= 0) & (r < count)
            mine = jnp.clip(r, 0, count - 1)
            coef = [
                [
                    jnp.broadcast_to(ops[t, k : k + 1, j : j + 1] * valid, (strip, width)).astype(jnp.bfloat16)
                    for j in range(states)
                ]
                for k in range(states)
            ]
            for a in range(0, width, strip):
                source = []
                for j in range(states):
                    value = extras[0][0, j, a : a + strip, :]
                    if len(extras) > 1:
                        value = jnp.where(halo <= 0, value, extras[1][0, j, a : a + strip, :])
                    source.append(jnp.where(inside, own[mine, j, a : a + strip, :], value))
                for k in range(states):
                    value = coef[k][0] * source[0]
                    for j in range(1, states):
                        value = value + coef[k][j] * source[j]
                    mixed[t % 2, a : a + strip, k * width : (k + 1) * width] = value
            value = jnp.dot(left[t, s], mixed[t % 2], preferred_element_type=jnp.float32)
            for k in range(states):
                inner[n % 2, k * width : (k + 1) * width, t * width : (t + 1) * width] = value[
                    :, k * width : (k + 1) * width
                ].astype(jnp.bfloat16)
        total[n % 2] = jnp.dot(
            inner[n % 2], rv[...].reshape(terms * width, width), preferred_element_type=jnp.float32
        ).astype(jnp.bfloat16)
    for place in range(devices):
        slot = jnp.where(odd == 1, orders[1][place], orders[0][place])
        target = (keep, send)[place // half]
        for n in range(len(blocks)):
            for k in range(states):
                first = pl.multiple_of(k * width + (slot ^ me) * rows, rows)
                target[place % half, n, k] = total[n % 2, pl.ds(first, rows), :]


def apply_blocks(blocks, facing, orders, couple, ops, left, right, own, extras, after):
    terms, width = right.shape[0], right.shape[1]
    states = own.shape[1]
    devices = len(orders[0])
    part = pltpu.VMEM((devices // 2, len(blocks), states, width // devices, width), jnp.bfloat16)
    vmem = pl.BlockSpec(memory_space=pltpu.VMEM)
    couple, ops, left = (pltpu.with_memory_space_constraint(v, pltpu.VMEM) for v in (couple, ops, left))
    pairs = len(blocks) * terms

    def body(*refs):
        used = 5 + len(extras)
        apply_body(blocks, facing, orders, *refs[:used], *refs[used + len(after) :])

    return pl.pallas_call(
        body,
        out_shape=[part] * 2,
        in_specs=[vmem] * (5 + len(extras) + len(after)),
        out_specs=[vmem] * 2,
        scratch_shapes=[
            pltpu.VMEM((2, width, states * width), jnp.bfloat16),
            pltpu.VMEM((min(2, len(blocks)), states * width, terms * width), jnp.bfloat16),
            pltpu.VMEM((min(2, len(blocks)), states * width, width), jnp.bfloat16),
        ],
        compiler_params=pltpu.CompilerParams(vmem_limit_bytes=VMEM_LIMIT),
        cost_estimate=pl.CostEstimate(
            flops=COST * 4 * pairs * states * width**3, bytes_accessed=pairs, transcendentals=0
        ),
        name=f"apply_{blocks[0][0]}",
    )(couple, ops, left, right, own, *extras, *after)


def finish_body(groups, live, *refs):
    refs, (out, done, sems) = refs[:-3], refs[-3:]
    odd, me = lax.axis_index("sec") % 2, lax.axis_index("term")
    own, states, rows, width = out.shape
    row = lax.broadcasted_iota(jnp.int32, (rows, width), 0) + me * rows
    col = lax.broadcasted_iota(jnp.int32, (rows, width), 1)
    copies = []
    for blocks in groups:
        last = blocks is groups[-1]
        terms, refs = (refs[:3], refs[3:]) if last else (refs[:1], refs[1:])
        for n, block in enumerate(blocks):
            s = jnp.where(odd == 1, block[1], block[0])
            size = entry(live[...].reshape(1, own), 0, s)
            ok = (row < size) & (col < size)
            at = len(copies)
            for k in range(states):
                value = terms[0][0, n, k].astype(jnp.float32)
                for term in terms[1:]:
                    value = value + term[0, n, k].astype(jnp.float32)
                done[at, k] = jnp.where(ok, value, 0.0).astype(jnp.bfloat16)
            copies.append(pltpu.make_async_copy(done.at[at], out.at[s], sems.at[at]))
            copies[-1].start()
    for copy in copies:
        copy.wait()


def finish(groups, live, parts, shape):
    vmem = pl.BlockSpec(memory_space=pltpu.VMEM)
    return pl.pallas_call(
        functools.partial(finish_body, groups),
        out_shape=pltpu.HBM(shape, jnp.bfloat16),
        in_specs=[vmem] * (1 + len(parts)),
        out_specs=pl.BlockSpec(memory_space=pltpu.HBM),
        scratch_shapes=[pltpu.VMEM(shape, jnp.bfloat16), pltpu.SemaphoreType.DMA((shape[0],))],
        compiler_params=pltpu.CompilerParams(vmem_limit_bytes=VMEM_LIMIT),
        name="finish",
    )(pltpu.with_memory_space_constraint(live, pltpu.VMEM), *parts)


def on_device(psi, left, right, ops, couple, live):
    secs, devices = lax.axis_size("sec"), lax.axis_size("term")
    own, states, width = psi.shape[0], psi.shape[1], psi.shape[2]

    bits = [1 << b for b in range(devices.bit_length() - 1)]
    routes = (bits, bits[::-1])
    orders = tuple(
        tuple(sorted(range(devices), key=lambda i: [bool(i & b) for b in route])) for route in routes
    )

    chip = [(i, i ^ 1) for i in range(secs)]
    psi, right, *sends = pick(psi, right)
    beyond = [lax.ppermute(v, "sec", chip) for v in sends[:2]]
    across = [over_link(sends[2], bits[0]), over_link(sends[3], bits[-1])]
    groups = (
        (((2, 1), (3, 0)), beyond),
        (((1, 2),), across[:1]),
        (((0, 3),), across),
    )
    sums, parts, after = [], [], []
    for g, (blocks, sources) in enumerate(groups):
        keep, send = apply_blocks(blocks, g == 0, orders, couple, ops, left, right, psi, sources, after)
        after = [keep]
        got = flip(send, routes, 0)
        for step in range(1, len(bits) - 1):
            half = keep.shape[0] // 2
            total = keep + got
            keep, send = total[:half], total[half:]
            got = flip(send, routes, step)
        send = keep[1:] + got[1:]
        parts = [keep[:1], got[:1], flip(send, routes, len(bits) - 1)]
        if g < len(groups) - 1:
            sums.append(sum(v.astype(jnp.float32) for v in parts).astype(jnp.bfloat16))
    shape = (own, states, width // devices, width)
    return finish(tuple(blocks for blocks, _ in groups), live, sums + parts, shape)


def solution(mesh):
    placed = (
        P("sec", None, None, None),
        P("term", "sec", None, None),
        P("term", None, None),
        P("term", None, None),
        P("term", "sec"),
        P("sec"),
    )
    return jax.shard_map(
        on_device,
        mesh=mesh,
        in_specs=placed,
        out_specs=P("sec", None, "term", None),
        check_vma=False,
    )
```

```python
import functools

import jax
import jax.numpy as jnp
from jax import lax
from jax.experimental import pallas as pl
from jax.experimental.pallas import tpu as pltpu
from jax.sharding import PartitionSpec as P

VMEM_LIMIT = 24 * 1024 * 1024
COST = 10
WAYS = (0, 0, 1)


def flip(value, routes, step):
    secs, devices = lax.axis_size("sec"), lax.axis_size("term")
    pairs = []
    for sec in range(secs):
        for term in range(devices):
            pairs.append((sec * devices + term, sec * devices + (term ^ routes[sec % 2][step])))
    return lax.ppermute(value, ("sec", "term"), pairs)


def over_link(value, bit):
    secs, devices = lax.axis_size("sec"), lax.axis_size("term")
    pairs = []
    for sec in range(secs):
        other = sec + 1 if sec % 2 else sec - 1
        for term in range(devices):
            to = other * devices + term if 0 <= other < secs else sec * devices + (term ^ bit)
            pairs.append((sec * devices + term, to))
    return lax.ppermute(value, ("sec", "term"), pairs)


def pick_body(psi, right, own, rv, *refs):
    outs, sems = refs[:-1], refs[-1]
    odd = lax.axis_index("sec") % 2
    copies = [pltpu.make_async_copy(psi, own, sems.at[0]), pltpu.make_async_copy(right, rv, sems.at[1])]
    for copy in copies:
        copy.start()
    copies[0].wait()
    last = psi.shape[0] - 1
    for out, even in zip(outs, (last, last - 1, 0, 1)):
        out[...] = own[pl.ds(jnp.where(odd == 1, last - even, even), 1)]
    copies[1].wait()


def pick(psi, right):
    vmem = pl.BlockSpec(memory_space=pltpu.VMEM)
    hbm = pl.BlockSpec(memory_space=pltpu.HBM)
    shapes = [pltpu.VMEM(psi.shape, psi.dtype), pltpu.VMEM(right.shape, right.dtype)]
    shapes += [pltpu.VMEM((1,) + psi.shape[1:], psi.dtype)] * 4
    return pl.pallas_call(
        pick_body,
        out_shape=shapes,
        in_specs=[hbm, hbm],
        out_specs=[vmem] * 6,
        scratch_shapes=[pltpu.SemaphoreType.DMA((2,))],
        compiler_params=pltpu.CompilerParams(vmem_limit_bytes=VMEM_LIMIT),
        name="pick",
    )(*(pltpu.with_memory_space_constraint(v, pltpu.HBM) for v in (psi, right)))


def entry(table, *at):
    here = True
    for axis, index in enumerate(at):
        here = here & (lax.broadcasted_iota(jnp.int32, table.shape, axis) == index)
    return jnp.sum(jnp.where(here, table.astype(jnp.float32), 0.0)).astype(jnp.int32)


def apply_body(blocks, facing, orders, couple, ops, left, rv, own, *refs):
    extras, (keep, send, mixed, inner, total) = refs[:-5], refs[-5:]
    terms, width = rv.shape[0], rv.shape[1]
    count, states = own.shape[0], own.shape[1]
    devices = len(orders[0])
    half = devices // 2
    rows = width // devices
    sec, me = lax.axis_index("sec"), lax.axis_index("term")
    base, odd = sec * count, sec % 2
    strip = 16

    for n, block in enumerate(blocks):
        s = jnp.where(odd == 1, block[1], block[0])
        for t in range(terms):
            c = entry(couple[...], t, s)
            valid = jnp.where(c >= 0, 1.0, 0.0).astype(jnp.float32)
            r = jnp.where(c >= 0, c - base, 0)
            halo = jnp.where((odd == 1) == facing, -1 - r, r - count)
            inside = (r >= 0) & (r < count)
            mine = jnp.clip(r, 0, count - 1)
            coef = [
                [
                    jnp.broadcast_to(ops[t, k : k + 1, j : j + 1] * valid, (strip, width)).astype(jnp.bfloat16)
                    for j in range(states)
                ]
                for k in range(states)
            ]
            for a in range(0, width, strip):
                source = []
                for j in range(states):
                    value = extras[0][0, j, a : a + strip, :]
                    if len(extras) > 1:
                        value = jnp.where(halo <= 0, value, extras[1][0, j, a : a + strip, :])
                    source.append(jnp.where(inside, own[mine, j, a : a + strip, :], value))
                for k in range(states):
                    value = coef[k][0] * source[0]
                    for j in range(1, states):
                        value = value + coef[k][j] * source[j]
                    mixed[t % 2, a : a + strip, k * width : (k + 1) * width] = value
            value = jnp.dot(left[t, s], mixed[t % 2], preferred_element_type=jnp.float32)
            for k in range(states):
                inner[n % 2, k * width : (k + 1) * width, t * width : (t + 1) * width] = value[
                    :, k * width : (k + 1) * width
                ].astype(jnp.bfloat16)
        total[n % 2] = jnp.dot(
            inner[n % 2], rv[...].reshape(terms * width, width), preferred_element_type=jnp.float32
        ).astype(jnp.bfloat16)
    for place in range(devices):
        slot = jnp.where(odd == 1, orders[1][place], orders[0][place])
        target = (keep, send)[place // half]
        for n in range(len(blocks)):
            for k in range(states):
                first = pl.multiple_of(k * width + (slot ^ me) * rows, rows)
                target[place % half, n, k] = total[n % 2, pl.ds(first, rows), :]


def apply_blocks(blocks, facing, orders, couple, ops, left, right, own, extras, after):
    terms, width = right.shape[0], right.shape[1]
    states = own.shape[1]
    devices = len(orders[0])
    part = pltpu.VMEM((devices // 2, len(blocks), states, width // devices, width), jnp.bfloat16)
    vmem = pl.BlockSpec(memory_space=pltpu.VMEM)
    couple, ops, left = (pltpu.with_memory_space_constraint(v, pltpu.VMEM) for v in (couple, ops, left))
    pairs = len(blocks) * terms

    def body(*refs):
        used = 5 + len(extras)
        apply_body(blocks, facing, orders, *refs[:used], *refs[used + len(after) :])

    return pl.pallas_call(
        body,
        out_shape=[part] * 2,
        in_specs=[vmem] * (5 + len(extras) + len(after)),
        out_specs=[vmem] * 2,
        scratch_shapes=[
            pltpu.VMEM((2, width, states * width), jnp.bfloat16),
            pltpu.VMEM((min(2, len(blocks)), states * width, terms * width), jnp.bfloat16),
            pltpu.VMEM((min(2, len(blocks)), states * width, width), jnp.bfloat16),
        ],
        compiler_params=pltpu.CompilerParams(vmem_limit_bytes=VMEM_LIMIT),
        cost_estimate=pl.CostEstimate(
            flops=COST * 4 * pairs * states * width**3, bytes_accessed=pairs, transcendentals=0
        ),
        name=f"apply_{blocks[0][0]}",
    )(couple, ops, left, right, own, *extras, *after)


def finish_body(groups, live, *refs):
    refs, (out, done, sems) = refs[:-3], refs[-3:]
    odd, me = lax.axis_index("sec") % 2, lax.axis_index("term")
    own, states, rows, width = out.shape
    row = lax.broadcasted_iota(jnp.int32, (rows, width), 0) + me * rows
    col = lax.broadcasted_iota(jnp.int32, (rows, width), 1)
    copies = []
    for blocks in groups:
        last = blocks is groups[-1]
        terms, refs = (refs[:3], refs[3:]) if last else (refs[:1], refs[1:])
        for n, block in enumerate(blocks):
            s = jnp.where(odd == 1, block[1], block[0])
            size = entry(live[...].reshape(1, own), 0, s)
            ok = (row < size) & (col < size)
            at = len(copies)
            for k in range(states):
                value = terms[0][0, n, k].astype(jnp.float32)
                for term in terms[1:]:
                    value = value + term[0, n, k].astype(jnp.float32)
                done[at, k] = jnp.where(ok, value, 0.0).astype(jnp.bfloat16)
            copies.append(pltpu.make_async_copy(done.at[at], out.at[s], sems.at[at]))
            copies[-1].start()
    for copy in copies:
        copy.wait()


def finish(groups, live, parts, shape):
    vmem = pl.BlockSpec(memory_space=pltpu.VMEM)
    return pl.pallas_call(
        functools.partial(finish_body, groups),
        out_shape=pltpu.HBM(shape, jnp.bfloat16),
        in_specs=[vmem] * (1 + len(parts)),
        out_specs=pl.BlockSpec(memory_space=pltpu.HBM),
        scratch_shapes=[pltpu.VMEM(shape, jnp.bfloat16), pltpu.SemaphoreType.DMA((shape[0],))],
        compiler_params=pltpu.CompilerParams(vmem_limit_bytes=VMEM_LIMIT),
        name="finish",
    )(pltpu.with_memory_space_constraint(live, pltpu.VMEM), *parts)


def on_device(psi, left, right, ops, couple, live):
    secs, devices = lax.axis_size("sec"), lax.axis_size("term")
    own, states, width = psi.shape[0], psi.shape[1], psi.shape[2]

    bits = [1 << b for b in range(devices.bit_length() - 1)]
    ways = ((bits, bits[::-1]), (bits[::-1], bits))

    chip = [(i, i ^ 1) for i in range(secs)]
    psi, right, *sends = pick(psi, right)
    beyond = [lax.ppermute(v, "sec", chip) for v in sends[:2]]
    across = [over_link(sends[2], bits[0]), over_link(sends[3], bits[-1])]
    groups = (
        (((2, 1), (3, 0)), beyond),
        (((1, 2),), across[:1]),
        (((0, 3),), across),
    )
    sums, parts, after = [], [], []
    for g, (blocks, sources) in enumerate(groups):
        routes = ways[WAYS[g]]
        orders = tuple(
            tuple(sorted(range(devices), key=lambda i: [bool(i & b) for b in route])) for route in routes
        )
        keep, send = apply_blocks(blocks, g == 0, orders, couple, ops, left, right, psi, sources, after)
        after = [keep]
        got = flip(send, routes, 0)
        for step in range(1, len(bits) - 1):
            half = keep.shape[0] // 2
            total = keep + got
            keep, send = total[:half], total[half:]
            got = flip(send, routes, step)
        send = keep[1:] + got[1:]
        parts = [keep[:1], got[:1], flip(send, routes, len(bits) - 1)]
        if g < len(groups) - 1:
            sums.append(sum(v.astype(jnp.float32) for v in parts).astype(jnp.bfloat16))
    shape = (own, states, width // devices, width)
    return finish(tuple(blocks for blocks, _ in groups), live, sums + parts, shape)


def solution(mesh):
    placed = (
        P("sec", None, None, None),
        P("term", "sec", None, None),
        P("term", None, None),
        P("term", None, None),
        P("term", "sec"),
        P("sec"),
    )
    return jax.shard_map(
        on_device,
        mesh=mesh,
        in_specs=placed,
        out_specs=P("sec", None, "term", None),
        check_vma=False,
    )
```

```python
import functools

import jax
import jax.numpy as jnp
from jax import lax
from jax.experimental import pallas as pl
from jax.experimental.pallas import tpu as pltpu
from jax.sharding import PartitionSpec as P

VMEM_LIMIT = 24 * 1024 * 1024
COST = 10
WAYS = (0, 0, 1)


def flip(value, routes, step):
    secs, devices = lax.axis_size("sec"), lax.axis_size("term")
    pairs = []
    for sec in range(secs):
        for term in range(devices):
            pairs.append((sec * devices + term, sec * devices + (term ^ routes[sec % 2][step])))
    return lax.ppermute(value, ("sec", "term"), pairs)


def over_link(value, bit):
    secs, devices = lax.axis_size("sec"), lax.axis_size("term")
    pairs = []
    for sec in range(secs):
        other = sec + 1 if sec % 2 else sec - 1
        for term in range(devices):
            to = other * devices + term if 0 <= other < secs else sec * devices + (term ^ bit)
            pairs.append((sec * devices + term, to))
    return lax.ppermute(value, ("sec", "term"), pairs)


def pick_body(psi, right, own, rv, *refs):
    outs, sems = refs[:-1], refs[-1]
    odd = lax.axis_index("sec") % 2
    copies = [pltpu.make_async_copy(psi, own, sems.at[0]), pltpu.make_async_copy(right, rv, sems.at[1])]
    for copy in copies:
        copy.start()
    copies[0].wait()
    last = psi.shape[0] - 1
    for out, even in zip(outs, (last, last - 1, 0, 1)):
        out[...] = own[pl.ds(jnp.where(odd == 1, last - even, even), 1)]
    copies[1].wait()


def pick(psi, right):
    vmem = pl.BlockSpec(memory_space=pltpu.VMEM)
    hbm = pl.BlockSpec(memory_space=pltpu.HBM)
    shapes = [pltpu.VMEM(psi.shape, psi.dtype), pltpu.VMEM(right.shape, right.dtype)]
    shapes += [pltpu.VMEM((1,) + psi.shape[1:], psi.dtype)] * 4
    return pl.pallas_call(
        pick_body,
        out_shape=shapes,
        in_specs=[hbm, hbm],
        out_specs=[vmem] * 6,
        scratch_shapes=[pltpu.SemaphoreType.DMA((2,))],
        compiler_params=pltpu.CompilerParams(vmem_limit_bytes=VMEM_LIMIT),
        name="pick",
    )(*(pltpu.with_memory_space_constraint(v, pltpu.HBM) for v in (psi, right)))


def entry(table, *at):
    here = True
    for axis, index in enumerate(at):
        here = here & (lax.broadcasted_iota(jnp.int32, table.shape, axis) == index)
    return jnp.sum(jnp.where(here, table.astype(jnp.float32), 0.0)).astype(jnp.int32)


def apply_body(blocks, facing, orders, couple, ops, left, rv, own, *refs):
    extras, (keep, send, mixed, inner, total) = refs[:-5], refs[-5:]
    terms, width = rv.shape[0], rv.shape[1]
    count, states = own.shape[0], own.shape[1]
    devices = len(orders[0])
    half = devices // 2
    rows = width // devices
    sec, me = lax.axis_index("sec"), lax.axis_index("term")
    base, odd = sec * count, sec % 2
    strip = 16

    for n, block in enumerate(blocks):
        s = jnp.where(odd == 1, block[1], block[0])
        for t in range(terms):
            c = entry(couple[...], t, s)
            valid = jnp.where(c >= 0, 1.0, 0.0).astype(jnp.float32)
            r = jnp.where(c >= 0, c - base, 0)
            halo = jnp.where((odd == 1) == facing, -1 - r, r - count)
            inside = (r >= 0) & (r < count)
            mine = jnp.clip(r, 0, count - 1)
            coef = [
                [
                    jnp.broadcast_to(ops[t, k : k + 1, j : j + 1] * valid, (strip, width)).astype(jnp.bfloat16)
                    for j in range(states)
                ]
                for k in range(states)
            ]
            for a in range(0, width, strip):
                source = []
                for j in range(states):
                    value = extras[0][0, j, a : a + strip, :]
                    if len(extras) > 1:
                        value = jnp.where(halo <= 0, value, extras[1][0, j, a : a + strip, :])
                    source.append(jnp.where(inside, own[mine, j, a : a + strip, :], value))
                for k in range(states):
                    value = coef[k][0] * source[0]
                    for j in range(1, states):
                        value = value + coef[k][j] * source[j]
                    mixed[t % 2, a : a + strip, k * width : (k + 1) * width] = value
            value = jnp.dot(left[t, s], mixed[t % 2], preferred_element_type=jnp.float32)
            for k in range(states):
                inner[n % 2, k * width : (k + 1) * width, t * width : (t + 1) * width] = value[
                    :, k * width : (k + 1) * width
                ].astype(jnp.bfloat16)
        total[n % 2] = jnp.dot(
            inner[n % 2], rv[...].reshape(terms * width, width), preferred_element_type=jnp.float32
        ).astype(jnp.bfloat16)
    for place in range(devices):
        slot = jnp.where(odd == 1, orders[1][place], orders[0][place])
        target = (keep, send)[place // half]
        for n in range(len(blocks)):
            for k in range(states):
                first = pl.multiple_of(k * width + (slot ^ me) * rows, rows)
                target[place % half, n, k] = total[n % 2, pl.ds(first, rows), :]


def apply_blocks(blocks, facing, orders, couple, ops, left, right, own, extras, after):
    terms, width = right.shape[0], right.shape[1]
    states = own.shape[1]
    devices = len(orders[0])
    part = pltpu.VMEM((devices // 2, len(blocks), states, width // devices, width), jnp.bfloat16)
    vmem = pl.BlockSpec(memory_space=pltpu.VMEM)
    couple, ops, left = (pltpu.with_memory_space_constraint(v, pltpu.VMEM) for v in (couple, ops, left))
    pairs = len(blocks) * terms

    def body(*refs):
        used = 5 + len(extras)
        apply_body(blocks, facing, orders, *refs[:used], *refs[used + len(after) :])

    return pl.pallas_call(
        body,
        out_shape=[part] * 2,
        in_specs=[vmem] * (5 + len(extras) + len(after)),
        out_specs=[vmem] * 2,
        scratch_shapes=[
            pltpu.VMEM((2, width, states * width), jnp.bfloat16),
            pltpu.VMEM((min(2, len(blocks)), states * width, terms * width), jnp.bfloat16),
            pltpu.VMEM((min(2, len(blocks)), states * width, width), jnp.bfloat16),
        ],
        compiler_params=pltpu.CompilerParams(vmem_limit_bytes=VMEM_LIMIT),
        cost_estimate=pl.CostEstimate(
            flops=COST * 4 * pairs * states * width**3, bytes_accessed=pairs, transcendentals=0
        ),
        name=f"apply_{blocks[0][0]}",
    )(couple, ops, left, right, own, *extras, *after)


def finish_body(groups, live, *refs):
    refs, (out, done, sems) = refs[:-3], refs[-3:]
    odd, me = lax.axis_index("sec") % 2, lax.axis_index("term")
    own, states, rows, width = out.shape
    row = lax.broadcasted_iota(jnp.int32, (rows, width), 0) + me * rows
    col = lax.broadcasted_iota(jnp.int32, (rows, width), 1)
    copies = []
    for blocks in groups:
        terms, refs = refs[:3], refs[3:]
        for n, block in enumerate(blocks):
            s = jnp.where(odd == 1, block[1], block[0])
            size = entry(live[...].reshape(1, own), 0, s)
            ok = (row < size) & (col < size)
            at = len(copies)
            for k in range(states):
                value = terms[0][0, n, k].astype(jnp.float32)
                for term in terms[1:]:
                    value = value + term[0, n, k].astype(jnp.float32)
                done[at, k] = jnp.where(ok, value, 0.0).astype(jnp.bfloat16)
            copies.append(pltpu.make_async_copy(done.at[at], out.at[s], sems.at[at]))
            copies[-1].start()
    for copy in copies:
        copy.wait()


def finish(groups, live, parts, shape):
    vmem = pl.BlockSpec(memory_space=pltpu.VMEM)
    return pl.pallas_call(
        functools.partial(finish_body, groups),
        out_shape=pltpu.HBM(shape, jnp.bfloat16),
        in_specs=[vmem] * (1 + len(parts)),
        out_specs=pl.BlockSpec(memory_space=pltpu.HBM),
        scratch_shapes=[pltpu.VMEM(shape, jnp.bfloat16), pltpu.SemaphoreType.DMA((shape[0],))],
        compiler_params=pltpu.CompilerParams(vmem_limit_bytes=VMEM_LIMIT),
        name="finish",
    )(pltpu.with_memory_space_constraint(live, pltpu.VMEM), *parts)


def on_device(psi, left, right, ops, couple, live):
    secs, devices = lax.axis_size("sec"), lax.axis_size("term")
    own, states, width = psi.shape[0], psi.shape[1], psi.shape[2]

    bits = [1 << b for b in range(devices.bit_length() - 1)]
    ways = ((bits, bits[::-1]), (bits[::-1], bits))

    chip = [(i, i ^ 1) for i in range(secs)]
    psi, right, *sends = pick(psi, right)
    beyond = [lax.ppermute(v, "sec", chip) for v in sends[:2]]
    across = [over_link(sends[2], bits[0]), over_link(sends[3], bits[-1])]
    groups = (
        (((2, 1), (3, 0)), beyond),
        (((1, 2),), across[:1]),
        (((0, 3),), across),
    )
    sums, parts, after = [], [], []
    for g, (blocks, sources) in enumerate(groups):
        routes = ways[WAYS[g]]
        orders = tuple(
            tuple(sorted(range(devices), key=lambda i: [bool(i & b) for b in route])) for route in routes
        )
        keep, send = apply_blocks(blocks, g == 0, orders, couple, ops, left, right, psi, sources, after)
        after = [keep]
        got = flip(send, routes, 0)
        for step in range(1, len(bits) - 1):
            half = keep.shape[0] // 2
            total = keep + got
            keep, send = total[:half], total[half:]
            got = flip(send, routes, step)
        send = keep[1:] + got[1:]
        parts = [keep[:1], got[:1], flip(send, routes, len(bits) - 1)]
        sums += parts
    shape = (own, states, width // devices, width)
    return finish(tuple(blocks for blocks, _ in groups), live, sums, shape)


def solution(mesh):
    placed = (
        P("sec", None, None, None),
        P("term", "sec", None, None),
        P("term", None, None),
        P("term", None, None),
        P("term", "sec"),
        P("sec"),
    )
    return jax.shard_map(
        on_device,
        mesh=mesh,
        in_specs=placed,
        out_specs=P("sec", None, "term", None),
        check_vma=False,
    )
```
